32 devices in a mesh: belt: 8 (over z, core), mer: 4 (over y, x).
Axes of the slice: x: 2, y: 2, z: 4, core: 2. Of those that a mesh axis runs over, the one named last changes fastest.
Arguments:
- right_side: float32 [120, 32, 6144], P(None, 'mer', 'belt')
- helm_diag: float32 [120, 32, 6144], P(None, 'mer', 'belt'), may hold values from 1 to 3
- east_coef: float32 [120, 32, 6144], P(None, 'mer', 'belt'), may hold values from 0.5 to 1.5
- north_coef: float32 [120, 32, 6144], P(None, 'mer', 'belt'), may hold values from 0.5 to 1.5
- vert_coef: float32 [119, 32, 6144], P(None, 'mer', 'belt'), may hold values from 100 to 1000
- mortar_weights: float32 [8, 2], replicated, may hold values from 0.25 to 2
- weight_index: int32 [4, 32], replicated, may hold values from 0 to 7
- edge_map: int32 [4, 32, 2], replicated, may hold values from 0 to 31, as said below
- refined: int32 [4, 32], replicated, may hold values 0 or 1
Outputs:
- solution: float32 [120, 32, 6144], P(None, 'mer', 'belt')
- residual: float32 [120, 32, 6144], P(None, 'mer', 'belt')
The draws below stay inside these ranges and needn't reach their ends.
Inputs may be any that keep to these rules, and one draw needn't show every extreme that they name: `edge_map`: for each edge and each of the two entries of a row, the 32 rows' entries form a permutation of the rows.
All inputs are finite; a program needn't handle non-finite values.
Results may differ from the reference program's by a relative error of at most 0.0003.
Values sent between devices are 32-bit elements; how exact they have to be, the bound alone decides.
A program may use at most 128 MiB of HBM per device.

```python
import math
import jax
import jax.numpy as jnp
from jax import lax

LEV = 120
ITERS = 2
NW = 8
NR = 32
NC = 6144


def draw_right_side(key, part):
    key_base, key_rows, key_cols, key_amp = jax.random.split(key, 4)
    level_pos = (jnp.arange(LEV, dtype=jnp.float32) + 0.5) / LEV
    profile = 1.0 + 0.6 * jnp.cos(math.pi * level_pos)
    base = jnp.clip(jax.random.normal(key_base, (LEV, NR, NC), jnp.float32), -4.0, 4.0)
    amplitude = 1.5 * jnp.clip(jax.random.normal(key_amp, (NR, NC), jnp.float32), -4.0, 4.0)
    total = 0.5 * base + amplitude[None, :, :] * profile[:, None, None]
    row_scale = jnp.exp(jax.random.uniform(key_rows, (NR,), jnp.float32, 0.0, math.log(10.0)))
    col_scale = jnp.exp(jax.random.uniform(key_cols, (NC,), jnp.float32, 0.0, math.log(10.0)))
    panel_pos = jnp.arange(NC, dtype=jnp.int32) % (NC // 4)
    near_edge = jnp.logical_or(panel_pos >= NC // 4 - 3, panel_pos <= 1)
    edge_boost = jnp.where(near_edge, 16.0, 1.0).astype(jnp.float32)
    col_scale = col_scale * edge_boost
    return (total * row_scale[None, :, None] * col_scale[None, None, :] * 0.1).astype(jnp.float32)


def draw_edge_map(key, part):
    edges_list = []
    for edge_num in range(4):
        slots = []
        for slot_num in range(2):
            slots.append(jax.random.permutation(jax.random.fold_in(key, 2 * edge_num + slot_num), NR).astype(jnp.int32))
        edges_list.append(jnp.stack(slots, axis=1))
    return jnp.stack(edges_list, axis=0)


def touch_ends(array, rng, smallest, largest):
    shape = array.shape
    index_at = [jax.random.randint(jax.random.fold_in(rng, axis), (), 0, shape[axis]) for axis in range(len(shape))]
    array = array.at[tuple(index_at)].set(smallest)
    longest = shape.index(max(shape))
    index_at[longest] = (index_at[longest] + 1) % shape[longest]
    return array.at[tuple(index_at)].set(largest)


def block_scale(own_key, extent, cuts, least, top_value):
    def one(position, parts):
        steps = jax.random.uniform(jax.random.fold_in(jax.random.fold_in(own_key, 6), position), (parts,), jnp.float32, least / len(cuts), top_value / len(cuts))
        return jnp.repeat(jnp.exp(steps), extent[position] // parts).reshape((-1,) + (1,) * (len(extent) - position - 1))

    factor_of = one(*cuts[0])
    for cut in cuts[1:]:
        factor_of = factor_of * one(*cut)
    return factor_of


def setup_inputs(seed: int = 0) -> dict:
    splits = jax.random.split(jax.random.key(seed), 10)
    return {
        "right_side": draw_right_side(jax.random.fold_in(splits[9], 71), 0),
        "helm_diag": jnp.clip(1.0 + 2.0 * jax.random.uniform(splits[1], (LEV, NR, NC), jnp.float32) ** block_scale(splits[1], (LEV, NR, NC), ((1, 4), (2, 8)), -0.2, 0.2), 1.0, 3.0),
        "east_coef": jnp.clip(0.5 + 1.0 * jax.random.uniform(splits[2], (LEV, NR, NC), jnp.float32) ** block_scale(splits[2], (LEV, NR, NC), ((1, 4), (2, 8)), -0.2, 0.2), 0.5, 1.5),
        "north_coef": jnp.clip(0.5 + 1.0 * jax.random.uniform(splits[3], (LEV, NR, NC), jnp.float32) ** block_scale(splits[3], (LEV, NR, NC), ((1, 4), (2, 8)), -0.2, 0.2), 0.5, 1.5),
        "vert_coef": jnp.clip(jnp.exp(math.log(1000.0) - 2.3025851 * jax.random.uniform(splits[4], (LEV - 1, NR, NC), jnp.float32) ** block_scale(splits[4], (LEV - 1, NR, NC), ((1, 4), (2, 8)), -0.2, 0.2)), 100.0, 1000.0),
        "mortar_weights": jnp.clip(jax.random.uniform(splits[5], (NW, 2), jnp.float32, 0.25, 2.0), 0.25, 2.0),
        "weight_index": touch_ends(jax.random.randint(splits[6], (4, NR), 0, NW), jax.random.fold_in(splits[6], 1), 0, NW - 1).astype(jnp.int32),
        "edge_map": draw_edge_map(jax.random.fold_in(splits[9], 71), 0),
        "refined": touch_ends((jax.random.randint(splits[8], (4, NR), 0, 2) < 1).astype(jnp.int32), jax.random.fold_in(splits[8], 1), 0, 1),
    }


def factor_columns(diagonal_sum, lower_coupling):
    def advance(previous, input_arrays):
        diag_level, lower_level = input_arrays
        ratio = lower_level / previous
        present_entry = diag_level - lower_level * ratio
        return present_entry, (1.0 / present_entry, ratio)
    start_value = jnp.ones_like(diagonal_sum[0])
    last_pivot, (inverse_pivot, ratio_values) = lax.scan(advance, start_value, (diagonal_sum, lower_coupling))
    return inverse_pivot, ratio_values


def solve_columns(values, inverse_pivot, ratio_values, upper_coupling):
    def forward(previous, input_arrays):
        value_level, ratio_layer = input_arrays
        present_entry = value_level + ratio_layer * previous
        return present_entry, present_entry
    zero_level = jnp.zeros_like(values[0])
    last_value, eliminated = lax.scan(forward, zero_level, (values, ratio_values))

    def backward(successor_entry, input_arrays):
        eliminated_layer, pivot_layer, upper_layer = input_arrays
        present_entry = pivot_layer * (eliminated_layer + upper_layer * successor_entry)
        return present_entry, present_entry
    first_value, solved = lax.scan(backward, zero_level, (eliminated, inverse_pivot, upper_coupling), reverse=True)
    return solved


def vertical_parts(vert_coef):
    zero_level = jnp.zeros((1,) + vert_coef.shape[1:], vert_coef.dtype)
    upper = jnp.concatenate([vert_coef, zero_level], axis=0)
    lower = jnp.concatenate([zero_level, vert_coef], axis=0)
    return upper, lower


def apply_operator(field, helm_diag, east_coef, west_coef, north_coef, south_coef, upper, lower,
                   edge_map, weight_index, mortar_weights, refined):
    panel = NC // 4
    east_side = jnp.roll(field, -1, axis=2)
    west_side = jnp.roll(field, 1, axis=2)
    for edge_num in range(4):
        west_col = (edge_num + 1) * panel - 1
        edge_rim = east_side[:, :, west_col]
        first_weight = mortar_weights[weight_index[edge_num], 0]
        second_weight = mortar_weights[weight_index[edge_num], 1]
        mortar = first_weight[None, :] * edge_rim[:, edge_map[edge_num, :, 0]] + second_weight[None, :] * edge_rim[:, edge_map[edge_num, :, 1]]
        east_side = east_side.at[:, :, west_col].set(jnp.where(refined[edge_num][None, :] == 1, mortar, edge_rim))
    zero_row = jnp.zeros((field.shape[0], 1, field.shape[2]), field.dtype)
    north_side = jnp.concatenate([field[:, 1:], zero_row], axis=1)
    south_side = jnp.concatenate([zero_row, field[:, :-1]], axis=1)
    zero_level = jnp.zeros((1,) + field.shape[1:], field.dtype)
    up_side = jnp.concatenate([field[1:], zero_level], axis=0)
    down_side = jnp.concatenate([zero_level, field[:-1]], axis=0)
    return (helm_diag * field + east_coef * (field - east_side) + west_coef * (field - west_side)
            + north_coef * (field - north_side) + south_coef * (field - south_side)
            + upper * (field - up_side) + lower * (field - down_side))


def reference(right_side, helm_diag, east_coef, north_coef, vert_coef, mortar_weights, weight_index, edge_map, refined):
    west_coef = jnp.roll(east_coef, 1, axis=2)
    zero_row = jnp.zeros((north_coef.shape[0], 1, north_coef.shape[2]), north_coef.dtype)
    south_coef = jnp.concatenate([zero_row, north_coef[:, :-1]], axis=1)
    upper, lower = vertical_parts(vert_coef)
    diagonal_sum = helm_diag + east_coef + west_coef + north_coef + south_coef + upper + lower
    inverse_pivot, ratio_values = factor_columns(diagonal_sum, lower)

    def operate(field):
        return apply_operator(field, helm_diag, east_coef, west_coef, north_coef, south_coef, upper, lower,
                              edge_map, weight_index, mortar_weights, refined)

    solution = jnp.zeros_like(right_side)
    residual = right_side
    precond = solve_columns(residual, inverse_pivot, ratio_values, upper)
    norm_now = jnp.sum(residual * precond)
    direction = precond
    for step_num in range(ITERS):
        image = operate(direction)
        step_size = norm_now / jnp.sum(direction * image)
        solution = solution + step_size * direction
        residual = residual - step_size * image
        if step_num + 1 < ITERS:
            precond = solve_columns(residual, inverse_pivot, ratio_values, upper)
            norm_next = jnp.sum(residual * precond)
            direction = precond + (norm_next / norm_now) * direction
            norm_now = norm_next
    return solution, residual
```

```python
import functools

import jax
import jax.numpy as jnp
from jax import lax
from jax.experimental import pallas as pl
from jax.experimental.pallas import tpu as pltpu
from jax.sharding import PartitionSpec as P

LANES = 128
F32 = jnp.float32
MESH = pl.DeviceIdType.MESH
UNROLL = 4


def kernel(
    B, M, NB,
    rs_h, he_h, ea_h, no_h, ve_h, mw, wi, em, rf,
    sol_h, res_h,
    rs, he, ea, no, ve, pf, wf, im, jm, uu, iv,
    crow_s, crow_r, row_s, row_r, ccol_s, ccol_r, colw_s, colw_r, cole_s, cole_r,
    red1, red2,
    loc_sem, out_sem, crow_ss, crow_rs, row_ss, row_rs, ccol_sem, colw_sem, cole_ss, cole_rs,
    red1_ss, red1_rs, red2_ss, red2_rs,
):
    lev, rows, cols = rs.shape
    width = cols // NB
    per = width // LANES
    total_rows = wi.shape[1]
    nblk = cols // LANES
    b = lax.axis_index("belt")
    m = lax.axis_index("mer")
    per_panel = B // 4
    east_b = lax.rem(b + 1, B)
    west_b = lax.rem(b + B - 1, B)
    lane = lax.broadcasted_iota(jnp.int32, (rows, LANES), 1)
    sub = lax.broadcasted_iota(jnp.int32, (rows, LANES), 0)
    first_lane, last_lane = lane == 0, lane == LANES - 1
    first_row, last_row = sub == 0, sub == rows - 1
    zero = jnp.zeros((rows, LANES), F32)

    def at(j):
        return pl.ds(j * LANES, LANES)

    barrier = pltpu.get_barrier_semaphore()
    count = 0
    for d in range(1, B):
        pl.semaphore_signal(barrier, inc=1, device_id=(lax.rem(b + d, B), m), device_id_type=MESH)
        count += 1
    for d in range(1, M):
        other = lax.rem(m + d, M)
        for target in (b, east_b, west_b):
            pl.semaphore_signal(barrier, inc=1, device_id=(target, other), device_id_type=MESH)
            count += 1

    def load(which, src, dst, c):
        lanes = pl.ds(c * width, width)
        n = src.shape[0]
        return pltpu.make_async_copy(
            src.at[:, :, lanes], dst.at[pl.ds(0, n), :, lanes], loc_sem.at[which, c]
        )

    def loads(c):
        return [load(2, he_h, he, c), load(3, ve_h, ve, c), load(4, rs_h, rs, c)]

    for c in range(NB):
        load(0, no_h, no, c).start()
    for c in [NB - 1] + list(range(NB - 1)):
        load(1, ea_h, ea, c).start()
    for c in range(NB):
        for copy in loads(c):
            copy.start()
    ve[lev - 1] = jnp.zeros((rows, cols), F32)

    @pl.when(m == 0)
    def _():
        crow_r[...] = jnp.zeros(crow_r.shape, F32)
        row_r[:, 0] = jnp.zeros((2,) + row_r.shape[2:], F32)

    @pl.when(m == M - 1)
    def _():
        row_r[:, 1] = jnp.zeros((2,) + row_r.shape[2:], F32)

    def coef_row(c):
        return pltpu.make_async_remote_copy(
            src_ref=crow_s.at[c], dst_ref=crow_r.at[c], send_sem=crow_ss.at[c], recv_sem=crow_rs.at[c],
            device_id=(b, lax.rem(m + 1, M)), device_id_type=MESH)

    def field_row(f, side, c):
        to = lax.rem(m + 1, M) if side == 0 else lax.rem(m + M - 1, M)
        return pltpu.make_async_remote_copy(
            src_ref=row_s.at[f, side, c], dst_ref=row_r.at[f, side, c],
            send_sem=row_ss.at[f, side, c], recv_sem=row_rs.at[f, side, c],
            device_id=(b, to), device_id_type=MESH)

    def sends(copies_up, copies_down, what):
        @pl.when(m < M - 1)
        def _():
            for copy in copies_up:
                getattr(copy, what)()

        @pl.when(m > 0)
        def _():
            for copy in copies_down:
                getattr(copy, what)()

    coef_col = pltpu.make_async_remote_copy(
        src_ref=ccol_s, dst_ref=ccol_r, send_sem=ccol_sem.at[0], recv_sem=ccol_sem.at[1],
        device_id=(east_b, m), device_id_type=MESH)

    def last_col(f):
        return pltpu.make_async_remote_copy(
            src_ref=colw_s.at[f], dst_ref=colw_r.at[f], send_sem=colw_sem.at[f, 0], recv_sem=colw_sem.at[f, 1],
            device_id=(east_b, m), device_id_type=MESH)

    def first_cols(f):
        copies = []
        for d in range(M):
            copies.append(pltpu.make_async_remote_copy(
                src_ref=cole_s.at[f], dst_ref=cole_r.at[f, m], send_sem=cole_ss.at[f, d], recv_sem=cole_rs.at[f, m],
                device_id=(west_b, lax.rem(m + d, M)), device_id_type=MESH))
        return copies

    def first_col_wait(f, d):
        src = lax.rem(m + d, M)
        pltpu.make_async_remote_copy(
            src_ref=cole_s.at[f], dst_ref=cole_r.at[f, src], send_sem=cole_ss.at[f, d], recv_sem=cole_rs.at[f, src],
            device_id=(west_b, m), device_id_type=MESH).wait_recv()

    def level_loop(body, carry, reverse=False):
        def step(i, carry):
            for u in range(UNROLL):
                k = i * UNROLL + u
                if reverse:
                    k = lev - 1 - k
                carry = body(k, carry)
            return carry
        return lax.fori_loop(0, lev // UNROLL, step, carry)

    load(1, ea_h, ea, NB - 1).wait()

    def pack_coef(k, acc):
        return jnp.where(lane == k, pltpu.roll(ea[k, :, at(nblk - 1)], k + 1, 1), acc)

    ccol_s[...] = level_loop(pack_coef, zero)
    started = False
    for c in range(NB):
        load(0, no_h, no, c).wait()

        def pack_rows(k, _, c=c):
            for j in range(per):
                crow_s[c, j, pl.ds(k, 1), :] = no[k, pl.ds(rows - 1, 1), at(c * per + j)]
            return 0

        level_loop(pack_rows, 0)
        if not started:
            pl.semaphore_wait(barrier, count)
            coef_col.start()
            started = True
        sends([coef_row(c)], [], "start")

    e = b // per_panel
    lane_r = lax.broadcasted_iota(jnp.int32, (rows, total_rows), 1)
    sub_r = lax.broadcasted_iota(jnp.int32, (rows, total_rows), 0)
    own = lane_r == sub_r + m * rows
    maps = em[pl.ds(e, 1), pl.ds(pl.multiple_of(m * rows, rows), rows), :][0]
    pick_row = jnp.broadcast_to(wi[pl.ds(e, 1), :].astype(F32), (rows, total_rows))
    flag_row = jnp.broadcast_to(rf[pl.ds(e, 1), :].astype(F32), (rows, total_rows))
    pick = jnp.sum(jnp.where(own, pick_row, 0.0), axis=1, keepdims=True)
    flag = jnp.sum(jnp.where(own, flag_row, 0.0), axis=1, keepdims=True)
    at_edge = jnp.where(lax.rem(b + 1, per_panel) == 0, 1.0, 0.0)
    weights = jnp.zeros((rows, 2), F32)
    for j in range(mw.shape[0]):
        weights = jnp.where(pick == float(j), mw[j:j + 1, :], weights)
    mortar = jnp.where(lane_r == maps[:, 0:1], weights[:, 0:1], 0.0) + jnp.where(
        lane_r == maps[:, 1:2], weights[:, 1:2], 0.0)
    mortar = jnp.where(flag * at_edge > 0.5, mortar, jnp.where(own, 1.0, 0.0))

    def arrived_col(f):
        for d in range(M):
            first_col_wait(f, d)
        out = zero
        for s in range(total_rows):
            out = out + mortar[:, s:s + 1] * cole_r[f, s // rows, s % rows:s % rows + 1, :]
        return out

    def row_of(ref, k, j):
        return jnp.broadcast_to(ref[j, pl.ds(k, 1), :], (rows, LANES))

    def solve_back(c, f, field, get, put, extra, extra_body):
        c0 = c * per

        def body(k, carry):
            prev, packs, more = carry
            cur = []
            for j in range(per):
                z = iv[k, :, at(c0 + j)] * get[k, :, at(c0 + j)] + uu[k, :, at(c0 + j)] * prev[j]
                put[k, :, at(c0 + j)] = z
                row_s[f, 0, c, j, pl.ds(k, 1), :] = z[rows - 1:rows]
                row_s[f, 1, c, j, pl.ds(k, 1), :] = z[0:1]
                cur.append(z)
            lo, hi = packs
            if c == 0:
                lo = jnp.where(lane == k, pltpu.roll(cur[0], k, 1), lo)
            if c == NB - 1:
                hi = jnp.where(lane == k, pltpu.roll(cur[-1], k + 1, 1), hi)
            return tuple(cur), (lo, hi), extra_body(k, cur, more)

        _, (lo, hi), more = level_loop(body, ((zero,) * per, (zero, zero), extra), reverse=True)
        if c == 0:
            cole_s[f] = lo
            for copy in first_cols(f):
                copy.start()
        if c == NB - 1:
            colw_s[f] = hi
            last_col(f).start()
        sends([field_row(f, 0, c)], [field_row(f, 1, c)], "start")
        return more

    for c in [NB - 1] + list(range(NB - 1)):
        if c != NB - 1:
            load(1, ea_h, ea, c).wait()
    coef_col.wait_recv()
    for c in range(NB):
        for copy in loads(c):
            copy.wait()

        @pl.when(m > 0)
        def _():
            coef_row(c).wait_recv()

        c0 = c * per

        def factor(k, carry, c=c, c0=c0):
            v_prev, u_prev, g_prev = carry
            v_cur, u_cur, g_cur = [], [], []
            east = [ea[k, :, at(c0 + j)] for j in range(per)]
            turned = [pltpu.roll(x, 1, 1) for x in east]
            if c == 0:
                before = pltpu.roll(ccol_r[...], LANES - k, 1)
            else:
                before = pltpu.roll(ea[k, :, at(c0 - 1)], 1, 1)
            for j in range(per):
                north = no[k, :, at(c0 + j)]
                west = jnp.where(first_lane, before if j == 0 else turned[j - 1], turned[j])
                south = jnp.where(first_row, row_of(crow_r.at[c], k, j), pltpu.roll(north, 1, 0))
                up = ve[k, :, at(c0 + j)]
                diag = he[k, :, at(c0 + j)] + east[j] + west + north + south + up + v_prev[j]
                pivot = diag - v_prev[j] * u_prev[j]
                inverse = 1.0 / pivot
                u = up * inverse
                g = rs[k, :, at(c0 + j)] + u_prev[j] * g_prev[j]
                iv[k, :, at(c0 + j)] = inverse
                uu[k, :, at(c0 + j)] = u
                pf[k, :, at(c0 + j)] = g
                v_cur.append(up)
                u_cur.append(u)
                g_cur.append(g)
            return tuple(v_cur), tuple(u_cur), tuple(g_cur)

        level_loop(factor, ((zero,) * per,) * 3)
        solve_back(c, 0, None, pf, pf, 0, lambda k, cur, more: more)

    def horizontal(f, field, k, c, east_halo, west_halo):
        c0 = c * per
        v = [field[k, :, at(c0 + j)] for j in range(per)]
        east = [ea[k, :, at(c0 + j)] for j in range(per)]
        ahead = [pltpu.roll(x, LANES - 1, 1) for x in v]
        if c == NB - 1:
            ahead.append(pltpu.roll(east_halo, LANES - 1 - k, 1))
        else:
            ahead.append(pltpu.roll(field[k, :, at(c0 + per)], LANES - 1, 1))
        behind = [pltpu.roll(x * y, 1, 1) for x, y in zip(v, east)]
        if c == 0:
            behind.insert(0, pltpu.roll(west_halo, LANES - k, 1))
        else:
            behind.insert(0, pltpu.roll(field[k, :, at(c0 - 1)] * ea[k, :, at(c0 - 1)], 1, 1))
        out = []
        for j in range(per):
            north = no[k, :, at(c0 + j)]
            e_side = jnp.where(last_lane, ahead[j + 1], ahead[j])
            w_term = jnp.where(first_lane, behind[j], behind[j + 1])
            n_side = jnp.where(last_row, row_of(row_r.at[f, 1, c], k, j), pltpu.roll(v[j], rows - 1, 0))
            s_halo = row_of(row_r.at[f, 0, c], k, j) * row_of(crow_r.at[c], k, j)
            s_term = jnp.where(first_row, s_halo, pltpu.roll(north * v[j], 1, 0))
            out.append(east[j] * e_side + w_term + north * n_side + s_term)
        return v, out

    def wait_rows(f, c):
        @pl.when(m > 0)
        def _():
            field_row(f, 0, c).wait_recv()

        @pl.when(m < M - 1)
        def _():
            field_row(f, 1, c).wait_recv()

    last_col(0).wait_recv()
    east_halo = arrived_col(0)
    west_halo = colw_r[0] * ccol_r[...]
    rz, a00, a10, a01, a11 = zero, zero, zero, zero, zero
    for c in range(NB):
        wait_rows(0, c)
        c0 = c * per

        def image(k, carry, c=c, c0=c0):
            u_prev, g_prev, rz, a00 = carry
            u_cur, g_cur = [], []
            v, h = horizontal(0, pf, k, c, east_halo, west_halo)
            for j in range(per):
                r = rs[k, :, at(c0 + j)]
                x = r - h[j]
                g = x + u_prev[j] * g_prev[j]
                im[k, :, at(c0 + j)] = x
                wf[k, :, at(c0 + j)] = g
                rz = rz + r * v[j]
                a00 = a00 + x * v[j]
                u_cur.append(uu[k, :, at(c0 + j)])
                g_cur.append(g)
            return tuple(u_cur), tuple(g_cur), rz, a00

        _, _, rz, a00 = level_loop(image, ((zero,) * per, (zero,) * per, rz, a00))

        def dot(k, cur, more, c0=c0):
            for j in range(per):
                more = more + cur[j] * im[k, :, at(c0 + j)]
            return more

        a10 = solve_back(c, 1, None, wf, wf, a10, dot)

    last_col(1).wait_recv()
    east_halo = arrived_col(1)
    west_halo = colw_r[1] * ccol_r[...]
    for c in range(NB):
        wait_rows(1, c)
        c0 = c * per

        def second(k, carry, c=c, c0=c0):
            a01, a11 = carry
            v, h = horizontal(1, wf, k, c, east_halo, west_halo)
            for j in range(per):
                x = im[k, :, at(c0 + j)] - h[j]
                jm[k, :, at(c0 + j)] = x
                a01 = a01 + x * pf[k, :, at(c0 + j)]
                a11 = a11 + x * v[j]
            return a01, a11

        a01, a11 = level_loop(second, (a01, a11))

    tile = zero
    for i, acc in enumerate((rz, a00, a10, a01, a11)):
        tile = jnp.where(sub == i, jnp.sum(acc, axis=0, keepdims=True), tile)

    def exchange(buf, size, me, dev, ss, rs_, tile):
        buf[me] = tile
        copies = []
        for d in range(1, size):
            copies.append(pltpu.make_async_remote_copy(
                src_ref=buf.at[me], dst_ref=buf.at[me], send_sem=ss.at[d], recv_sem=rs_.at[me],
                device_id=dev(lax.rem(me + d, size)), device_id_type=MESH))
        for copy in copies:
            copy.start()
        for d in range(1, size):
            src = lax.rem(me + d, size)
            pltpu.make_async_remote_copy(
                src_ref=buf.at[me], dst_ref=buf.at[src], send_sem=ss.at[d], recv_sem=rs_.at[src],
                device_id=dev(src), device_id_type=MESH).wait_recv()
        out = buf[0]
        for i in range(1, size):
            out = out + buf[i]
        return out, copies

    tile, copies1 = exchange(red1, B, b, lambda i: (i, m), red1_ss, red1_rs, tile)
    tile, copies2 = exchange(red2, M, m, lambda i: (b, i), red2_ss, red2_rs, tile)
    sums = jnp.sum(tile, axis=1, keepdims=True)
    rz, a00, a10, a01, a11 = (sums[i:i + 1] for i in range(5))
    step0 = rz / a00
    rz1 = rz - 2.0 * step0 * a00 + step0 * step0 * a10
    grow = 1.0 + rz1 / rz
    curve = grow * grow * a00 - grow * step0 * (a01 + a10) + step0 * step0 * a11
    step1 = rz1 / curve
    along = jnp.broadcast_to(step0 + step1 * grow, (rows, LANES))
    back = jnp.broadcast_to(step1 * step0, (rows, LANES))

    outs = []
    for c in range(NB):
        c0 = c * per

        def finish(k, _, c0=c0):
            for j in range(per):
                s = at(c0 + j)
                iv[k, :, s] = along * pf[k, :, s] - back * wf[k, :, s]
                uu[k, :, s] = rs[k, :, s] - along * im[k, :, s] + back * jm[k, :, s]
            return 0

        level_loop(finish, 0)
        lanes = pl.ds(c * width, width)
        for i, (src, dst) in enumerate(((iv, sol_h), (uu, res_h))):
            copy = pltpu.make_async_copy(src.at[:, :, lanes], dst.at[:, :, lanes], out_sem.at[i, c])
            copy.start()
            outs.append(copy)

    coef_col.wait_send()
    for f in range(2):
        last_col(f).wait_send()
        for copy in first_cols(f):
            copy.wait_send()
    for c in range(NB):
        sends([coef_row(c), field_row(0, 0, c), field_row(1, 0, c)],
              [field_row(0, 1, c), field_row(1, 1, c)], "wait_send")
    for copy in copies1 + copies2:
        copy.wait_send()
    for copy in outs:
        copy.wait()


def on_device(B, M, right_side, helm_diag, east_coef, north_coef, vert_coef,
              mortar_weights, weight_index, edge_map, refined):
    lev, rows, cols = right_side.shape
    NB = 3
    width = cols // NB
    any_spec = pl.BlockSpec(memory_space=pl.ANY)
    vmem = pl.BlockSpec(memory_space=pltpu.VMEM)
    whole = pltpu.VMEM((lev, rows, cols), F32)
    tile = (rows, LANES)
    dma = pltpu.SemaphoreType.DMA
    return pl.pallas_call(
        functools.partial(kernel, B, M, NB),
        out_shape=(jax.ShapeDtypeStruct(right_side.shape, F32),) * 2,
        in_specs=[any_spec] * 5 + [vmem] * 4,
        out_specs=(any_spec, any_spec),
        scratch_shapes=[whole] * 11 + [
            pltpu.VMEM((NB, width // LANES, lev, LANES), F32),
            pltpu.VMEM((NB, width // LANES, lev, LANES), F32),
            pltpu.VMEM((2, 2, NB, width // LANES, lev, LANES), F32),
            pltpu.VMEM((2, 2, NB, width // LANES, lev, LANES), F32),
            pltpu.VMEM(tile, F32),
            pltpu.VMEM(tile, F32),
            pltpu.VMEM((2,) + tile, F32),
            pltpu.VMEM((2,) + tile, F32),
            pltpu.VMEM((2,) + tile, F32),
            pltpu.VMEM((2, M) + tile, F32),
            pltpu.VMEM((B,) + tile, F32),
            pltpu.VMEM((M,) + tile, F32),
            dma((5, NB)), dma((2, NB)), dma((NB,)), dma((NB,)), dma((2, 2, NB)), dma((2, 2, NB)),
            dma((2,)), dma((2, 2)), dma((2, M)), dma((2, M)),
            dma((B,)), dma((B,)), dma((M,)), dma((M,)),
        ],
        compiler_params=pltpu.CompilerParams(
            collective_id=0, has_side_effects=True, vmem_limit_bytes=56 * 1024 * 1024),
        cost_estimate=pl.CostEstimate(flops=60 * lev * rows * cols, bytes_accessed=28 * lev * rows * cols,
                                      transcendentals=0),
    )(right_side, helm_diag, east_coef, north_coef, vert_coef, mortar_weights, weight_index, edge_map, refined)


def solution(mesh):
    split = P(None, "mer", "belt")
    return jax.shard_map(
        functools.partial(on_device, mesh.shape["belt"], mesh.shape["mer"]),
        mesh=mesh,
        in_specs=(split,) * 5 + (P(),) * 4,
        out_specs=(split, split),
        check_vma=False,
    )
```

```python
import functools

import jax
import jax.numpy as jnp
from jax import lax
from jax.experimental import pallas as pl
from jax.experimental.pallas import tpu as pltpu
from jax.sharding import PartitionSpec as P

LANES = 128
F32 = jnp.float32
MESH = pl.DeviceIdType.MESH
UNROLL = 24


def kernel(
    B, M, NB,
    rs_h, he_h, ea_h, no_h, ve_h, mw, wi, em, rf,
    sol_h, res_h,
    rs, he, ea, no, ve, pf, wf, im, jm, uu, iv,
    crow_s, crow_r, row_s, row_r, ccol_s, ccol_r, colw_s, colw_r, cole_s, cole_r,
    red1, red2,
    loc_sem, out_sem, crow_ss, crow_rs, row_ss, row_rs, ccol_sem, colw_sem, cole_ss, cole_rs,
    red1_ss, red1_rs, red2_ss, red2_rs,
):
    lev, rows, cols = rs.shape
    width = cols // NB
    per = width // LANES
    total_rows = wi.shape[1]
    nblk = cols // LANES
    b = lax.axis_index("belt")
    m = lax.axis_index("mer")
    per_panel = B // 4
    east_b = lax.rem(b + 1, B)
    west_b = lax.rem(b + B - 1, B)
    lane = lax.broadcasted_iota(jnp.int32, (rows, LANES), 1)
    sub = lax.broadcasted_iota(jnp.int32, (rows, LANES), 0)
    first_lane, last_lane = lane == 0, lane == LANES - 1
    first_row, last_row = sub == 0, sub == rows - 1
    zero = jnp.zeros((rows, LANES), F32)

    def at(j):
        return pl.ds(j * LANES, LANES)

    barrier = pltpu.get_barrier_semaphore()
    count = 0
    for d in range(1, B):
        pl.semaphore_signal(barrier, inc=1, device_id=(lax.rem(b + d, B), m), device_id_type=MESH)
        count += 1
    for d in range(1, M):
        other = lax.rem(m + d, M)
        for target in (b, east_b, west_b):
            pl.semaphore_signal(barrier, inc=1, device_id=(target, other), device_id_type=MESH)
            count += 1

    def load(which, src, dst, c):
        lanes = pl.ds(c * width, width)
        n = src.shape[0]
        return pltpu.make_async_copy(
            src.at[:, :, lanes], dst.at[pl.ds(0, n), :, lanes], loc_sem.at[which, c]
        )

    def loads(c):
        return [load(2, he_h, he, c), load(3, ve_h, ve, c), load(4, rs_h, rs, c)]

    for c in range(NB):
        load(0, no_h, no, c).start()
    for c in [NB - 1] + list(range(NB - 1)):
        load(1, ea_h, ea, c).start()
    for c in range(NB):
        for copy in loads(c):
            copy.start()
    ve[lev - 1] = jnp.zeros((rows, cols), F32)

    @pl.when(m == 0)
    def _():
        crow_r[...] = jnp.zeros(crow_r.shape, F32)
        row_r[:, 0] = jnp.zeros((2,) + row_r.shape[2:], F32)

    @pl.when(m == M - 1)
    def _():
        row_r[:, 1] = jnp.zeros((2,) + row_r.shape[2:], F32)

    def coef_row(c):
        return pltpu.make_async_remote_copy(
            src_ref=crow_s.at[c], dst_ref=crow_r.at[c], send_sem=crow_ss.at[c], recv_sem=crow_rs.at[c],
            device_id=(b, lax.rem(m + 1, M)), device_id_type=MESH)

    def field_row(f, side, c):
        to = lax.rem(m + 1, M) if side == 0 else lax.rem(m + M - 1, M)
        return pltpu.make_async_remote_copy(
            src_ref=row_s.at[f, side, c], dst_ref=row_r.at[f, side, c],
            send_sem=row_ss.at[f, side, c], recv_sem=row_rs.at[f, side, c],
            device_id=(b, to), device_id_type=MESH)

    def sends(copies_up, copies_down, what):
        @pl.when(m < M - 1)
        def _():
            for copy in copies_up:
                getattr(copy, what)()

        @pl.when(m > 0)
        def _():
            for copy in copies_down:
                getattr(copy, what)()

    coef_col = pltpu.make_async_remote_copy(
        src_ref=ccol_s, dst_ref=ccol_r, send_sem=ccol_sem.at[0], recv_sem=ccol_sem.at[1],
        device_id=(east_b, m), device_id_type=MESH)

    def last_col(f):
        return pltpu.make_async_remote_copy(
            src_ref=colw_s.at[f], dst_ref=colw_r.at[f], send_sem=colw_sem.at[f, 0], recv_sem=colw_sem.at[f, 1],
            device_id=(east_b, m), device_id_type=MESH)

    def first_cols(f):
        copies = []
        for d in range(M):
            copies.append(pltpu.make_async_remote_copy(
                src_ref=cole_s.at[f], dst_ref=cole_r.at[f, m], send_sem=cole_ss.at[f, d], recv_sem=cole_rs.at[f, m],
                device_id=(west_b, lax.rem(m + d, M)), device_id_type=MESH))
        return copies

    def first_col_wait(f, d):
        src = lax.rem(m + d, M)
        pltpu.make_async_remote_copy(
            src_ref=cole_s.at[f], dst_ref=cole_r.at[f, src], send_sem=cole_ss.at[f, d], recv_sem=cole_rs.at[f, src],
            device_id=(west_b, m), device_id_type=MESH).wait_recv()

    def level_loop(body, carry, reverse=False):
        def step(i, carry):
            for u in range(UNROLL):
                k = i * UNROLL + u
                if reverse:
                    k = lev - 1 - k
                carry = body(k, carry)
            return carry
        return lax.fori_loop(0, lev // UNROLL, step, carry)

    load(1, ea_h, ea, NB - 1).wait()

    def pack_coef(k, acc):
        return jnp.where(lane == k, pltpu.roll(ea[k, :, at(nblk - 1)], k + 1, 1), acc)

    ccol_s[...] = level_loop(pack_coef, zero)
    started = False
    for c in range(NB):
        load(0, no_h, no, c).wait()

        def pack_rows(k, _, c=c):
            for j in range(per):
                crow_s[c, j, pl.ds(k, 1), :] = no[k, pl.ds(rows - 1, 1), at(c * per + j)]
            return 0

        level_loop(pack_rows, 0)
        if not started:
            pl.semaphore_wait(barrier, count)
            coef_col.start()
            started = True
        sends([coef_row(c)], [], "start")

    e = b // per_panel
    lane_r = lax.broadcasted_iota(jnp.int32, (rows, total_rows), 1)
    sub_r = lax.broadcasted_iota(jnp.int32, (rows, total_rows), 0)
    own = lane_r == sub_r + m * rows
    def own_entry(line):
        line = jnp.broadcast_to(line.astype(F32), (rows, total_rows))
        return jnp.sum(jnp.where(own, line, 0.0), axis=1, keepdims=True)

    maps = em[pl.ds(e, 1), :, :][0]
    first_map, second_map = own_entry(maps[0:1]), own_entry(maps[1:2])
    pick = own_entry(wi[pl.ds(e, 1), :])
    flag = own_entry(rf[pl.ds(e, 1), :])
    at_edge = jnp.where(lax.rem(b + 1, per_panel) == 0, 1.0, 0.0)
    entries = mw.shape[1]
    picked = pick == lax.broadcasted_iota(jnp.int32, (rows, entries), 1).astype(F32)
    weights = [
        jnp.sum(jnp.where(picked, jnp.broadcast_to(mw[i:i + 1, :], (rows, entries)), 0.0), axis=1, keepdims=True)
        for i in range(2)
    ]
    lane_f = lane_r.astype(F32)
    mortar = jnp.where(lane_f == first_map, weights[0], 0.0) + jnp.where(lane_f == second_map, weights[1], 0.0)
    mortar = jnp.where(flag * at_edge > 0.5, mortar, jnp.where(own, 1.0, 0.0))

    def arrived_col(f):
        for d in range(M):
            first_col_wait(f, d)
        out = zero
        for s in range(total_rows):
            out = out + mortar[:, s:s + 1] * cole_r[f, s // rows, s % rows:s % rows + 1, :]
        return out

    def row_of(ref, k, j):
        return jnp.broadcast_to(ref[j, pl.ds(k, 1), :], (rows, LANES))

    def solve_back(c, f, field, get, put, extra, extra_body):
        c0 = c * per

        def body(k, carry):
            prev, packs, more = carry
            cur = []
            for j in range(per):
                z = iv[k, :, at(c0 + j)] * get[k, :, at(c0 + j)] + uu[k, :, at(c0 + j)] * prev[j]
                put[k, :, at(c0 + j)] = z
                row_s[f, 0, c, j, pl.ds(k, 1), :] = z[rows - 1:rows]
                row_s[f, 1, c, j, pl.ds(k, 1), :] = z[0:1]
                cur.append(z)
            lo, hi = packs
            if c == 0:
                lo = jnp.where(lane == k, pltpu.roll(cur[0], k, 1), lo)
            if c == NB - 1:
                hi = jnp.where(lane == k, pltpu.roll(cur[-1], k + 1, 1), hi)
            return tuple(cur), (lo, hi), extra_body(k, cur, more)

        _, (lo, hi), more = level_loop(body, ((zero,) * per, (zero, zero), extra), reverse=True)
        if c == 0:
            cole_s[f] = lo
            for copy in first_cols(f):
                copy.start()
        if c == NB - 1:
            colw_s[f] = hi
            last_col(f).start()
        sends([field_row(f, 0, c)], [field_row(f, 1, c)], "start")
        return more

    for c in [NB - 1] + list(range(NB - 1)):
        if c != NB - 1:
            load(1, ea_h, ea, c).wait()
    coef_col.wait_recv()
    for c in range(NB):
        for copy in loads(c):
            copy.wait()

        @pl.when(m > 0)
        def _():
            coef_row(c).wait_recv()

        c0 = c * per

        def factor(k, carry, c=c, c0=c0):
            v_prev, u_prev, g_prev = carry
            v_cur, u_cur, g_cur = [], [], []
            east = [ea[k, :, at(c0 + j)] for j in range(per)]
            turned = [pltpu.roll(x, 1, 1) for x in east]
            if c == 0:
                before = pltpu.roll(ccol_r[...], LANES - k, 1)
            else:
                before = pltpu.roll(ea[k, :, at(c0 - 1)], 1, 1)
            for j in range(per):
                north = no[k, :, at(c0 + j)]
                west = jnp.where(first_lane, before if j == 0 else turned[j - 1], turned[j])
                south = jnp.where(first_row, row_of(crow_r.at[c], k, j), pltpu.roll(north, 1, 0))
                up = ve[k, :, at(c0 + j)]
                diag = he[k, :, at(c0 + j)] + east[j] + west + north + south + up + v_prev[j]
                pivot = diag - v_prev[j] * u_prev[j]
                inverse = 1.0 / pivot
                u = up * inverse
                g = rs[k, :, at(c0 + j)] + u_prev[j] * g_prev[j]
                iv[k, :, at(c0 + j)] = inverse
                uu[k, :, at(c0 + j)] = u
                pf[k, :, at(c0 + j)] = g
                v_cur.append(up)
                u_cur.append(u)
                g_cur.append(g)
            return tuple(v_cur), tuple(u_cur), tuple(g_cur)

        level_loop(factor, ((zero,) * per,) * 3)
        solve_back(c, 0, None, pf, pf, 0, lambda k, cur, more: more)

    def horizontal(f, field, k, c, east_halo, west_halo):
        c0 = c * per
        v = [field[k, :, at(c0 + j)] for j in range(per)]
        east = [ea[k, :, at(c0 + j)] for j in range(per)]
        ahead = [pltpu.roll(x, LANES - 1, 1) for x in v]
        if c == NB - 1:
            ahead.append(pltpu.roll(east_halo, LANES - 1 - k, 1))
        else:
            ahead.append(pltpu.roll(field[k, :, at(c0 + per)], LANES - 1, 1))
        behind = [pltpu.roll(x * y, 1, 1) for x, y in zip(v, east)]
        if c == 0:
            behind.insert(0, pltpu.roll(west_halo, LANES - k, 1))
        else:
            behind.insert(0, pltpu.roll(field[k, :, at(c0 - 1)] * ea[k, :, at(c0 - 1)], 1, 1))
        out = []
        for j in range(per):
            north = no[k, :, at(c0 + j)]
            e_side = jnp.where(last_lane, ahead[j + 1], ahead[j])
            w_term = jnp.where(first_lane, behind[j], behind[j + 1])
            n_side = jnp.where(last_row, row_of(row_r.at[f, 1, c], k, j), pltpu.roll(v[j], rows - 1, 0))
            s_halo = row_of(row_r.at[f, 0, c], k, j) * row_of(crow_r.at[c], k, j)
            s_term = jnp.where(first_row, s_halo, pltpu.roll(north * v[j], 1, 0))
            out.append(east[j] * e_side + w_term + north * n_side + s_term)
        return v, out

    def wait_rows(f, c):
        @pl.when(m > 0)
        def _():
            field_row(f, 0, c).wait_recv()

        @pl.when(m < M - 1)
        def _():
            field_row(f, 1, c).wait_recv()

    last_col(0).wait_recv()
    east_halo = arrived_col(0)
    west_halo = colw_r[0] * ccol_r[...]
    rz, a00, a10, a01, a11 = zero, zero, zero, zero, zero
    for c in range(NB):
        wait_rows(0, c)
        c0 = c * per

        def image(k, carry, c=c, c0=c0):
            u_prev, g_prev, rz, a00 = carry
            u_cur, g_cur = [], []
            v, h = horizontal(0, pf, k, c, east_halo, west_halo)
            for j in range(per):
                r = rs[k, :, at(c0 + j)]
                x = r - h[j]
                g = x + u_prev[j] * g_prev[j]
                im[k, :, at(c0 + j)] = x
                wf[k, :, at(c0 + j)] = g
                rz = rz + r * v[j]
                a00 = a00 + x * v[j]
                u_cur.append(uu[k, :, at(c0 + j)])
                g_cur.append(g)
            return tuple(u_cur), tuple(g_cur), rz, a00

        _, _, rz, a00 = level_loop(image, ((zero,) * per, (zero,) * per, rz, a00))

        def dot(k, cur, more, c0=c0):
            for j in range(per):
                more = more + cur[j] * im[k, :, at(c0 + j)]
            return more

        a10 = solve_back(c, 1, None, wf, wf, a10, dot)

    last_col(1).wait_recv()
    east_halo = arrived_col(1)
    west_halo = colw_r[1] * ccol_r[...]
    for c in range(NB):
        wait_rows(1, c)
        c0 = c * per

        def second(k, carry, c=c, c0=c0):
            a01, a11 = carry
            v, h = horizontal(1, wf, k, c, east_halo, west_halo)
            for j in range(per):
                x = im[k, :, at(c0 + j)] - h[j]
                jm[k, :, at(c0 + j)] = x
                a01 = a01 + x * pf[k, :, at(c0 + j)]
                a11 = a11 + x * v[j]
            return a01, a11

        a01, a11 = level_loop(second, (a01, a11))

    tile = zero
    for i, acc in enumerate((rz, a00, a10, a01, a11)):
        tile = jnp.where(sub == i, jnp.sum(acc, axis=0, keepdims=True), tile)

    def exchange(buf, size, me, dev, ss, rs_, tile):
        buf[me] = tile
        copies = []
        for d in range(1, size):
            copies.append(pltpu.make_async_remote_copy(
                src_ref=buf.at[me], dst_ref=buf.at[me], send_sem=ss.at[d], recv_sem=rs_.at[me],
                device_id=dev(lax.rem(me + d, size)), device_id_type=MESH))
        for copy in copies:
            copy.start()
        for d in range(1, size):
            src = lax.rem(me + d, size)
            pltpu.make_async_remote_copy(
                src_ref=buf.at[me], dst_ref=buf.at[src], send_sem=ss.at[d], recv_sem=rs_.at[src],
                device_id=dev(src), device_id_type=MESH).wait_recv()
        out = buf[0]
        for i in range(1, size):
            out = out + buf[i]
        return out, copies

    tile, copies1 = exchange(red1, B, b, lambda i: (i, m), red1_ss, red1_rs, tile)
    tile, copies2 = exchange(red2, M, m, lambda i: (b, i), red2_ss, red2_rs, tile)
    sums = jnp.sum(tile, axis=1, keepdims=True)
    rz, a00, a10, a01, a11 = (sums[i:i + 1] for i in range(5))
    step0 = rz / a00
    rz1 = rz - 2.0 * step0 * a00 + step0 * step0 * a10
    grow = 1.0 + rz1 / rz
    curve = grow * grow * a00 - grow * step0 * (a01 + a10) + step0 * step0 * a11
    step1 = rz1 / curve
    along = jnp.broadcast_to(step0 + step1 * grow, (rows, LANES))
    back = jnp.broadcast_to(step1 * step0, (rows, LANES))

    outs = []
    for c in range(NB):
        c0 = c * per

        def finish(k, _, c0=c0):
            for j in range(per):
                s = at(c0 + j)
                iv[k, :, s] = along * pf[k, :, s] - back * wf[k, :, s]
                uu[k, :, s] = rs[k, :, s] - along * im[k, :, s] + back * jm[k, :, s]
            return 0

        level_loop(finish, 0)
        lanes = pl.ds(c * width, width)
        for i, (src, dst) in enumerate(((iv, sol_h), (uu, res_h))):
            copy = pltpu.make_async_copy(src.at[:, :, lanes], dst.at[:, :, lanes], out_sem.at[i, c])
            copy.start()
            outs.append(copy)

    coef_col.wait_send()
    for f in range(2):
        last_col(f).wait_send()
        for copy in first_cols(f):
            copy.wait_send()
    for c in range(NB):
        sends([coef_row(c), field_row(0, 0, c), field_row(1, 0, c)],
              [field_row(0, 1, c), field_row(1, 1, c)], "wait_send")
    for copy in copies1 + copies2:
        copy.wait_send()
    for copy in outs:
        copy.wait()


def on_device(B, M, right_side, helm_diag, east_coef, north_coef, vert_coef,
              mortar_weights, weight_index, edge_map, refined):
    lev, rows, cols = right_side.shape
    NB = 2
    width = cols // NB
    any_spec = pl.BlockSpec(memory_space=pl.ANY)
    vmem = pl.BlockSpec(memory_space=pltpu.VMEM)
    whole = pltpu.VMEM((lev, rows, cols), F32)
    tile = (rows, LANES)
    dma = pltpu.SemaphoreType.DMA
    return pl.pallas_call(
        functools.partial(kernel, B, M, NB),
        out_shape=(jax.ShapeDtypeStruct(right_side.shape, F32),) * 2,
        in_specs=[any_spec] * 5 + [vmem] * 4,
        out_specs=(any_spec, any_spec),
        scratch_shapes=[whole] * 11 + [
            pltpu.VMEM((NB, width // LANES, lev, LANES), F32),
            pltpu.VMEM((NB, width // LANES, lev, LANES), F32),
            pltpu.VMEM((2, 2, NB, width // LANES, lev, LANES), F32),
            pltpu.VMEM((2, 2, NB, width // LANES, lev, LANES), F32),
            pltpu.VMEM(tile, F32),
            pltpu.VMEM(tile, F32),
            pltpu.VMEM((2,) + tile, F32),
            pltpu.VMEM((2,) + tile, F32),
            pltpu.VMEM((2,) + tile, F32),
            pltpu.VMEM((2, M) + tile, F32),
            pltpu.VMEM((B,) + tile, F32),
            pltpu.VMEM((M,) + tile, F32),
            dma((5, NB)), dma((2, NB)), dma((NB,)), dma((NB,)), dma((2, 2, NB)), dma((2, 2, NB)),
            dma((2,)), dma((2, 2)), dma((2, M)), dma((2, M)),
            dma((B,)), dma((B,)), dma((M,)), dma((M,)),
        ],
        compiler_params=pltpu.CompilerParams(
            collective_id=0, has_side_effects=True, vmem_limit_bytes=56 * 1024 * 1024),
        cost_estimate=pl.CostEstimate(flops=60 * lev * rows * cols, bytes_accessed=28 * lev * rows * cols,
                                      transcendentals=0),
    )(right_side, helm_diag, east_coef, north_coef, vert_coef,
      mortar_weights.T, weight_index, edge_map.transpose(0, 2, 1), refined)


def solution(mesh):
    split = P(None, "mer", "belt")
    return jax.shard_map(
        functools.partial(on_device, mesh.shape["belt"], mesh.shape["mer"]),
        mesh=mesh,
        in_specs=(split,) * 5 + (P(),) * 4,
        out_specs=(split, split),
        check_vma=False,
    )
```

```python
import functools

import jax
import jax.numpy as jnp
from jax import lax
from jax.experimental import pallas as pl
from jax.experimental.pallas import tpu as pltpu
from jax.sharding import PartitionSpec as P

LANES = 128
F32 = jnp.float32
MESH = pl.DeviceIdType.MESH
UNROLL = 24


def kernel(
    B, M, NB,
    rs_h, he_h, ea_h, no_h, ve_h, mw, wi, em, rf,
    sol_h, res_h,
    rs, he, ea, no, ve, pf, wf, im, jm, uu, iv,
    crow_s, crow_r, row_s, row_r, ccol_s, ccol_r, colw_s, colw_r, cole_s, cole_r,
    red1, red2, rel,
    loc_sem, out_sem, crow_ss, crow_rs, row_ss, row_rs, ccol_sem, colw_sem, cole_ss, cole_rs,
    red1_ss, red1_rs, red2_ss, red2_rs, rel_ss, rel_rs,
):
    lev, rows, cols = rs.shape
    width = cols // NB
    per = width // LANES
    total_rows = wi.shape[1]
    nblk = cols // LANES
    b = lax.axis_index("belt")
    m = lax.axis_index("mer")
    per_panel = B // 4
    east_b = lax.rem(b + 1, B)
    west_b = lax.rem(b + B - 1, B)
    lane = lax.broadcasted_iota(jnp.int32, (rows, LANES), 1)
    sub = lax.broadcasted_iota(jnp.int32, (rows, LANES), 0)
    first_lane, last_lane = lane == 0, lane == LANES - 1
    first_row, last_row = sub == 0, sub == rows - 1
    zero = jnp.zeros((rows, LANES), F32)

    def at(j):
        return pl.ds(j * LANES, LANES)

    barrier = pltpu.get_barrier_semaphore()
    count = 0
    for d in range(1, B):
        pl.semaphore_signal(barrier, inc=1, device_id=(lax.rem(b + d, B), m), device_id_type=MESH)
        count += 1
    for d in range(1, M):
        other = lax.rem(m + d, M)
        for target in (b, east_b, west_b):
            pl.semaphore_signal(barrier, inc=1, device_id=(target, other), device_id_type=MESH)
            count += 1

    def load(which, src, dst, c):
        lanes = pl.ds(c * width, width)
        n = src.shape[0]
        return pltpu.make_async_copy(
            src.at[:, :, lanes], dst.at[pl.ds(0, n), :, lanes], loc_sem.at[which, c]
        )

    def loads(c):
        return [load(2, he_h, he, c), load(3, ve_h, ve, c), load(4, rs_h, rs, c)]

    for c in range(NB):
        load(0, no_h, no, c).start()
    for c in [NB - 1] + list(range(NB - 1)):
        load(1, ea_h, ea, c).start()
    for c in range(NB):
        for copy in loads(c):
            copy.start()
    ve[lev - 1] = jnp.zeros((rows, cols), F32)

    @pl.when(m == 0)
    def _():
        crow_r[...] = jnp.zeros(crow_r.shape, F32)
        row_r[:, 0] = jnp.zeros((2,) + row_r.shape[2:], F32)

    @pl.when(m == M - 1)
    def _():
        row_r[:, 1] = jnp.zeros((2,) + row_r.shape[2:], F32)

    def coef_row(c):
        return pltpu.make_async_remote_copy(
            src_ref=crow_s.at[c], dst_ref=crow_r.at[c], send_sem=crow_ss.at[c], recv_sem=crow_rs.at[c],
            device_id=(b, lax.rem(m + 1, M)), device_id_type=MESH)

    def field_row(f, side, c):
        to = lax.rem(m + 1, M) if side == 0 else lax.rem(m + M - 1, M)
        return pltpu.make_async_remote_copy(
            src_ref=row_s.at[f, side, c], dst_ref=row_r.at[f, side, c],
            send_sem=row_ss.at[f, side, c], recv_sem=row_rs.at[f, side, c],
            device_id=(b, to), device_id_type=MESH)

    def sends(copies_up, copies_down, what):
        @pl.when(m < M - 1)
        def _():
            for copy in copies_up:
                getattr(copy, what)()

        @pl.when(m > 0)
        def _():
            for copy in copies_down:
                getattr(copy, what)()

    square = M == 4

    def relayed(i, c):
        return square and c == (NB - 1 if i == 0 else 0)

    def to_corner(i, src, send_sem, corner):
        return pltpu.make_async_remote_copy(
            src_ref=src, dst_ref=rel.at[i], send_sem=send_sem, recv_sem=rel_rs.at[i],
            device_id=(b, corner), device_id_type=MESH)

    def from_corner(i, side):
        c = NB - 1 if i == 0 else 0
        dst = crow_r.at[c] if i == 0 else row_r.at[i - 1, side, c]
        sem = crow_rs.at[c] if i == 0 else row_rs.at[i - 1, side, c]
        return pltpu.make_async_remote_copy(
            src_ref=rel.at[i], dst_ref=dst, send_sem=rel_ss.at[i], recv_sem=sem,
            device_id=(b, 2 - side), device_id_type=MESH)

    def forward(i, what):
        if not square:
            return
        for side in range(1 if i == 0 else 2):
            @pl.when(m == (3 if side == 0 else 0))
            def _():
                copy = from_corner(i, side)
                if what == "start":
                    to_corner(i, rel.at[i], rel_ss.at[i], 1).wait_recv()
                getattr(copy, what)()

    def start_coef(c):
        if not relayed(0, c):
            sends([coef_row(c)], [], "start")
            return

        @pl.when((m < M - 1) & (m != 1))
        def _():
            coef_row(c).start()

        @pl.when(m == 1)
        def _():
            to_corner(0, crow_s.at[c], crow_ss.at[c], 3).start()

    def start_rows(f, c):
        if not relayed(f + 1, c):
            sends([field_row(f, 0, c)], [field_row(f, 1, c)], "start")
            return

        for side, corner in ((0, 3), (1, 0)):
            @pl.when((m != 1 + side) & (m != corner))
            def _():
                field_row(f, side, c).start()

            @pl.when(m == 1 + side)
            def _():
                to_corner(f + 1, row_s.at[f, side, c], row_ss.at[f, side, c], corner).start()

    coef_col = pltpu.make_async_remote_copy(
        src_ref=ccol_s, dst_ref=ccol_r, send_sem=ccol_sem.at[0], recv_sem=ccol_sem.at[1],
        device_id=(east_b, m), device_id_type=MESH)

    def last_col(f):
        return pltpu.make_async_remote_copy(
            src_ref=colw_s.at[f], dst_ref=colw_r.at[f], send_sem=colw_sem.at[f, 0], recv_sem=colw_sem.at[f, 1],
            device_id=(east_b, m), device_id_type=MESH)

    def first_cols(f):
        copies = []
        for d in range(M):
            copies.append(pltpu.make_async_remote_copy(
                src_ref=cole_s.at[f], dst_ref=cole_r.at[f, m], send_sem=cole_ss.at[f, d], recv_sem=cole_rs.at[f, m],
                device_id=(west_b, lax.rem(m + d, M)), device_id_type=MESH))
        return copies

    def first_col_wait(f, d):
        src = lax.rem(m + d, M)
        pltpu.make_async_remote_copy(
            src_ref=cole_s.at[f], dst_ref=cole_r.at[f, src], send_sem=cole_ss.at[f, d], recv_sem=cole_rs.at[f, src],
            device_id=(west_b, m), device_id_type=MESH).wait_recv()

    def level_loop(body, carry, reverse=False):
        def step(i, carry):
            for u in range(UNROLL):
                k = i * UNROLL + u
                if reverse:
                    k = lev - 1 - k
                carry = body(k, carry)
            return carry
        return lax.fori_loop(0, lev // UNROLL, step, carry)

    load(1, ea_h, ea, NB - 1).wait()

    def pack_coef(k, acc):
        return jnp.where(lane == k, pltpu.roll(ea[k, :, at(nblk - 1)], k + 1, 1), acc)

    ccol_s[...] = level_loop(pack_coef, zero)
    started = False
    for c in range(NB):
        load(0, no_h, no, c).wait()

        def pack_rows(k, _, c=c):
            for j in range(per):
                crow_s[c, j, pl.ds(k, 1), :] = no[k, pl.ds(rows - 1, 1), at(c * per + j)]
            return 0

        level_loop(pack_rows, 0)
        if not started:
            pl.semaphore_wait(barrier, count)
            coef_col.start()
            started = True
        start_coef(c)

    e = b // per_panel
    lane_r = lax.broadcasted_iota(jnp.int32, (rows, total_rows), 1)
    sub_r = lax.broadcasted_iota(jnp.int32, (rows, total_rows), 0)
    own = lane_r == sub_r + m * rows
    def own_entry(line):
        line = jnp.broadcast_to(line.astype(F32), (rows, total_rows))
        return jnp.sum(jnp.where(own, line, 0.0), axis=1, keepdims=True)

    maps = em[pl.ds(e, 1), :, :][0]
    first_map, second_map = own_entry(maps[0:1]), own_entry(maps[1:2])
    pick = own_entry(wi[pl.ds(e, 1), :])
    flag = own_entry(rf[pl.ds(e, 1), :])
    at_edge = jnp.where(lax.rem(b + 1, per_panel) == 0, 1.0, 0.0)
    entries = mw.shape[1]
    picked = pick == lax.broadcasted_iota(jnp.int32, (rows, entries), 1).astype(F32)
    weights = [
        jnp.sum(jnp.where(picked, jnp.broadcast_to(mw[i:i + 1, :], (rows, entries)), 0.0), axis=1, keepdims=True)
        for i in range(2)
    ]
    lane_f = lane_r.astype(F32)
    mortar = jnp.where(lane_f == first_map, weights[0], 0.0) + jnp.where(lane_f == second_map, weights[1], 0.0)
    mortar = jnp.where(flag * at_edge > 0.5, mortar, jnp.where(own, 1.0, 0.0))

    def arrived_col(f):
        for d in range(M):
            first_col_wait(f, d)
        out = zero
        for s in range(total_rows):
            out = out + mortar[:, s:s + 1] * cole_r[f, s // rows, s % rows:s % rows + 1, :]
        return out

    def row_of(ref, k, j):
        return jnp.broadcast_to(ref[j, pl.ds(k, 1), :], (rows, LANES))

    def solve_back(c, f, field, get, put, extra, extra_body):
        c0 = c * per

        def body(k, carry):
            prev, packs, more = carry
            cur = []
            for j in range(per):
                z = iv[k, :, at(c0 + j)] * get[k, :, at(c0 + j)] + uu[k, :, at(c0 + j)] * prev[j]
                put[k, :, at(c0 + j)] = z
                row_s[f, 0, c, j, pl.ds(k, 1), :] = z[rows - 1:rows]
                row_s[f, 1, c, j, pl.ds(k, 1), :] = z[0:1]
                cur.append(z)
            lo, hi = packs
            if c == 0:
                lo = jnp.where(lane == k, pltpu.roll(cur[0], k, 1), lo)
            if c == NB - 1:
                hi = jnp.where(lane == k, pltpu.roll(cur[-1], k + 1, 1), hi)
            return tuple(cur), (lo, hi), extra_body(k, cur, more)

        _, (lo, hi), more = level_loop(body, ((zero,) * per, (zero, zero), extra), reverse=True)
        if c == 0:
            cole_s[f] = lo
            for copy in first_cols(f):
                copy.start()
        if c == NB - 1:
            colw_s[f] = hi
            last_col(f).start()
        start_rows(f, c)
        return more

    for c in [NB - 1] + list(range(NB - 1)):
        if c != NB - 1:
            load(1, ea_h, ea, c).wait()
    coef_col.wait_recv()
    for c in range(NB):
        for copy in loads(c):
            copy.wait()
        if c == NB - 1:
            forward(0, "start")

        @pl.when(m > 0)
        def _():
            coef_row(c).wait_recv()

        c0 = c * per

        def factor(k, carry, c=c, c0=c0):
            v_prev, u_prev, g_prev = carry
            v_cur, u_cur, g_cur = [], [], []
            east = [ea[k, :, at(c0 + j)] for j in range(per)]
            turned = [pltpu.roll(x, 1, 1) for x in east]
            if c == 0:
                before = pltpu.roll(ccol_r[...], LANES - k, 1)
            else:
                before = pltpu.roll(ea[k, :, at(c0 - 1)], 1, 1)
            for j in range(per):
                north = no[k, :, at(c0 + j)]
                west = jnp.where(first_lane, before if j == 0 else turned[j - 1], turned[j])
                south = jnp.where(first_row, row_of(crow_r.at[c], k, j), pltpu.roll(north, 1, 0))
                up = ve[k, :, at(c0 + j)]
                diag = he[k, :, at(c0 + j)] + east[j] + west + north + south + up + v_prev[j]
                pivot = diag - v_prev[j] * u_prev[j]
                inverse = 1.0 / pivot
                u = up * inverse
                g = rs[k, :, at(c0 + j)] + u_prev[j] * g_prev[j]
                iv[k, :, at(c0 + j)] = inverse
                uu[k, :, at(c0 + j)] = u
                pf[k, :, at(c0 + j)] = g
                v_cur.append(up)
                u_cur.append(u)
                g_cur.append(g)
            return tuple(v_cur), tuple(u_cur), tuple(g_cur)

        level_loop(factor, ((zero,) * per,) * 3)
        solve_back(c, 0, None, pf, pf, 0, lambda k, cur, more: more)

    def horizontal(f, field, k, c, east_halo, west_halo):
        c0 = c * per
        v = [field[k, :, at(c0 + j)] for j in range(per)]
        east = [ea[k, :, at(c0 + j)] for j in range(per)]
        ahead = [pltpu.roll(x, LANES - 1, 1) for x in v]
        if c == NB - 1:
            ahead.append(pltpu.roll(east_halo, LANES - 1 - k, 1))
        else:
            ahead.append(pltpu.roll(field[k, :, at(c0 + per)], LANES - 1, 1))
        behind = [pltpu.roll(x * y, 1, 1) for x, y in zip(v, east)]
        if c == 0:
            behind.insert(0, pltpu.roll(west_halo, LANES - k, 1))
        else:
            behind.insert(0, pltpu.roll(field[k, :, at(c0 - 1)] * ea[k, :, at(c0 - 1)], 1, 1))
        out = []
        for j in range(per):
            north = no[k, :, at(c0 + j)]
            e_side = jnp.where(last_lane, ahead[j + 1], ahead[j])
            w_term = jnp.where(first_lane, behind[j], behind[j + 1])
            n_side = jnp.where(last_row, row_of(row_r.at[f, 1, c], k, j), pltpu.roll(v[j], rows - 1, 0))
            s_halo = row_of(row_r.at[f, 0, c], k, j) * row_of(crow_r.at[c], k, j)
            s_term = jnp.where(first_row, s_halo, pltpu.roll(north * v[j], 1, 0))
            out.append(east[j] * e_side + w_term + north * n_side + s_term)
        return v, out

    def wait_rows(f, c):
        @pl.when(m > 0)
        def _():
            field_row(f, 0, c).wait_recv()

        @pl.when(m < M - 1)
        def _():
            field_row(f, 1, c).wait_recv()

    forward(1, "start")

    last_col(0).wait_recv()
    east_halo = arrived_col(0)
    west_halo = colw_r[0] * ccol_r[...]
    rz, a00, a10, a01, a11 = zero, zero, zero, zero, zero
    for c in range(NB):
        wait_rows(0, c)
        c0 = c * per

        def image(k, carry, c=c, c0=c0):
            u_prev, g_prev, rz, a00 = carry
            u_cur, g_cur = [], []
            v, h = horizontal(0, pf, k, c, east_halo, west_halo)
            for j in range(per):
                r = rs[k, :, at(c0 + j)]
                x = r - h[j]
                g = x + u_prev[j] * g_prev[j]
                im[k, :, at(c0 + j)] = x
                wf[k, :, at(c0 + j)] = g
                rz = rz + r * v[j]
                a00 = a00 + x * v[j]
                u_cur.append(uu[k, :, at(c0 + j)])
                g_cur.append(g)
            return tuple(u_cur), tuple(g_cur), rz, a00

        _, _, rz, a00 = level_loop(image, ((zero,) * per, (zero,) * per, rz, a00))

        def dot(k, cur, more, c0=c0):
            for j in range(per):
                more = more + cur[j] * im[k, :, at(c0 + j)]
            return more

        a10 = solve_back(c, 1, None, wf, wf, a10, dot)

    forward(2, "start")

    last_col(1).wait_recv()
    east_halo = arrived_col(1)
    west_halo = colw_r[1] * ccol_r[...]
    for c in range(NB):
        wait_rows(1, c)
        c0 = c * per

        def second(k, carry, c=c, c0=c0):
            a01, a11 = carry
            v, h = horizontal(1, wf, k, c, east_halo, west_halo)
            for j in range(per):
                x = im[k, :, at(c0 + j)] - h[j]
                jm[k, :, at(c0 + j)] = x
                a01 = a01 + x * pf[k, :, at(c0 + j)]
                a11 = a11 + x * v[j]
            return a01, a11

        a01, a11 = level_loop(second, (a01, a11))

    tile = zero
    for i, acc in enumerate((rz, a00, a10, a01, a11)):
        tile = jnp.where(sub == i, jnp.sum(acc, axis=0, keepdims=True), tile)

    def exchange(buf, size, me, dev, ss, rs_, tile):
        buf[me] = tile
        copies = []
        for d in range(1, size):
            copies.append(pltpu.make_async_remote_copy(
                src_ref=buf.at[me], dst_ref=buf.at[me], send_sem=ss.at[d], recv_sem=rs_.at[me],
                device_id=dev(lax.rem(me + d, size)), device_id_type=MESH))
        for copy in copies:
            copy.start()
        for d in range(1, size):
            src = lax.rem(me + d, size)
            pltpu.make_async_remote_copy(
                src_ref=buf.at[me], dst_ref=buf.at[src], send_sem=ss.at[d], recv_sem=rs_.at[src],
                device_id=dev(src), device_id_type=MESH).wait_recv()
        out = buf[0]
        for i in range(1, size):
            out = out + buf[i]
        return out, copies

    tile, copies1 = exchange(red1, B, b, lambda i: (i, m), red1_ss, red1_rs, tile)
    tile, copies2 = exchange(red2, M, m, lambda i: (b, i), red2_ss, red2_rs, tile)
    sums = jnp.sum(tile, axis=1, keepdims=True)
    rz, a00, a10, a01, a11 = (sums[i:i + 1] for i in range(5))
    step0 = rz / a00
    rz1 = rz - 2.0 * step0 * a00 + step0 * step0 * a10
    grow = 1.0 + rz1 / rz
    curve = grow * grow * a00 - grow * step0 * (a01 + a10) + step0 * step0 * a11
    step1 = rz1 / curve
    along = jnp.broadcast_to(step0 + step1 * grow, (rows, LANES))
    back = jnp.broadcast_to(step1 * step0, (rows, LANES))

    outs = []
    for c in range(NB):
        c0 = c * per

        def finish(k, _, c0=c0):
            for j in range(per):
                s = at(c0 + j)
                iv[k, :, s] = along * pf[k, :, s] - back * wf[k, :, s]
                uu[k, :, s] = rs[k, :, s] - along * im[k, :, s] + back * jm[k, :, s]
            return 0

        level_loop(finish, 0)
        lanes = pl.ds(c * width, width)
        for i, (src, dst) in enumerate(((iv, sol_h), (uu, res_h))):
            copy = pltpu.make_async_copy(src.at[:, :, lanes], dst.at[:, :, lanes], out_sem.at[i, c])
            copy.start()
            outs.append(copy)

    coef_col.wait_send()
    for f in range(2):
        last_col(f).wait_send()
        for copy in first_cols(f):
            copy.wait_send()
    for c in range(NB):
        sends([coef_row(c), field_row(0, 0, c), field_row(1, 0, c)],
              [field_row(0, 1, c), field_row(1, 1, c)], "wait_send")
    for i in range(3):
        forward(i, "wait_send")
    for copy in copies1 + copies2:
        copy.wait_send()
    for copy in outs:
        copy.wait()


def on_device(B, M, right_side, helm_diag, east_coef, north_coef, vert_coef,
              mortar_weights, weight_index, edge_map, refined):
    lev, rows, cols = right_side.shape
    NB = 2
    width = cols // NB
    any_spec = pl.BlockSpec(memory_space=pl.ANY)
    vmem = pl.BlockSpec(memory_space=pltpu.VMEM)
    whole = pltpu.VMEM((lev, rows, cols), F32)
    tile = (rows, LANES)
    dma = pltpu.SemaphoreType.DMA
    return pl.pallas_call(
        functools.partial(kernel, B, M, NB),
        out_shape=(jax.ShapeDtypeStruct(right_side.shape, F32),) * 2,
        in_specs=[any_spec] * 5 + [vmem] * 4,
        out_specs=(any_spec, any_spec),
        scratch_shapes=[whole] * 11 + [
            pltpu.VMEM((NB, width // LANES, lev, LANES), F32),
            pltpu.VMEM((NB, width // LANES, lev, LANES), F32),
            pltpu.VMEM((2, 2, NB, width // LANES, lev, LANES), F32),
            pltpu.VMEM((2, 2, NB, width // LANES, lev, LANES), F32),
            pltpu.VMEM(tile, F32),
            pltpu.VMEM(tile, F32),
            pltpu.VMEM((2,) + tile, F32),
            pltpu.VMEM((2,) + tile, F32),
            pltpu.VMEM((2,) + tile, F32),
            pltpu.VMEM((2, M) + tile, F32),
            pltpu.VMEM((B,) + tile, F32),
            pltpu.VMEM((M,) + tile, F32),
            pltpu.VMEM((3, width // LANES, lev, LANES), F32),
            dma((5, NB)), dma((2, NB)), dma((NB,)), dma((NB,)), dma((2, 2, NB)), dma((2, 2, NB)),
            dma((2,)), dma((2, 2)), dma((2, M)), dma((2, M)),
            dma((B,)), dma((B,)), dma((M,)), dma((M,)), dma((3,)), dma((3,)),
        ],
        compiler_params=pltpu.CompilerParams(
            collective_id=0, has_side_effects=True, vmem_limit_bytes=56 * 1024 * 1024),
        cost_estimate=pl.CostEstimate(flops=60 * lev * rows * cols, bytes_accessed=28 * lev * rows * cols,
                                      transcendentals=0),
    )(right_side, helm_diag, east_coef, north_coef, vert_coef,
      mortar_weights.T, weight_index, edge_map.transpose(0, 2, 1), refined)


def solution(mesh):
    split = P(None, "mer", "belt")
    return jax.shard_map(
        functools.partial(on_device, mesh.shape["belt"], mesh.shape["mer"]),
        mesh=mesh,
        in_specs=(split,) * 5 + (P(),) * 4,
        out_specs=(split, split),
        check_vma=False,
    )
```
